32 devices in a mesh: day: 2 (over y), chan: 16 (over z, x, core).
Axes of the slice: x: 2, y: 2, z: 4, core: 2. Of those that a mesh axis runs over, the one named last changes fastest.
Arguments:
- traces: bfloat16 [2560, 16, 1500], P(('day', 'chan')), parts along dimension 0, may hold values from -6 to 6
- quality: int32 [2560, 16], P(('day', 'chan')), parts along dimension 0, may hold values 0 or 1
- reach: int32 [2560], P(('day', 'chan')), parts along dimension 0, may hold values from 0 to 160
Outputs:
- correlations: bfloat16 [2560, 161, 201], P(('day', 'chan')), parts along dimension 0
The draws below stay inside these ranges and needn't reach their ends.
There are 2 independent parts, one for each index of `day`. The reference program is written for one: setup_inputs(seed, part) draws one part's arguments, and reference() takes and returns one part's arrays. A program takes and returns all parts, laid end to end along the dimension named above; each array names one. Nothing has to cross between parts.
All inputs are finite; a program needn't handle non-finite values. No bound on the sum of `quality` on one device may be relied on, other than what follows from the above.
Results may differ from the reference program's by a relative error of at most 0.0059.
Values may be sent and summed in bfloat16 or wider, within the bound.
A program may use at most 128 MiB of HBM per device.

```python
import math
import jax
import jax.numpy as jnp
from jax import lax

CH_DEV = 80
R = 160
W = 16
S = 1500
F = 256
HALF_SMOOTH = 32
LARGEST_LAG_SPAN = 100
FREQ_BLOCK = 128
C = 1280


def plant(entries, own_key, least, high):
    longest = entries.shape.index(max(entries.shape))
    spots = []
    for shift in (0, 1):
        where = [jax.random.randint(jax.random.fold_in(own_key, axis), (), 0, length) for axis, length in enumerate(entries.shape)]
        where[longest] = (where[longest] + shift) % entries.shape[longest]
        spots.append(tuple(where))
    return entries.at[spots[0]].set(least).at[spots[1]].set(high)


def shard_levels(rng, shape, split, low, top_value):
    loudness = 1.0
    for dim, parts in split:
        heights = jax.random.uniform(jax.random.fold_in(jax.random.fold_in(rng, 6), dim), (parts,), jnp.float32, low / len(split), top_value / len(split))
        loudness = loudness * jnp.repeat(jnp.exp(heights), shape[dim] // parts).reshape((-1,) + (1,) * (len(shape) - 1 - dim))
    return loudness


def gaussian(stream_key, extent, width, most, pieces=(), held_as=jnp.bfloat16):
    values = jax.random.normal(stream_key, extent, jnp.float32) * width
    if len(pieces) > 0:
        values = shard_levels(stream_key, extent, pieces, -0.22, 0.18) * values
    return jnp.clip(values, min=-most, max=most).astype(held_as)


def setup_inputs(seed: int = 0, part: int = 0) -> dict:
    keys = jax.random.split(jax.random.key(seed), 4)
    own_keys = jax.random.split(jax.random.fold_in(keys[3], part), 4)
    return {
        "traces": gaussian(own_keys[0], (C, W, S), 1.0, 6.0, ((0, 16),)),
        "quality": plant((jax.random.randint(own_keys[1], (C, W), 0, 8) < 7).astype(jnp.int32), jax.random.fold_in(own_keys[1], 1), 0, 1),
        "reach": plant(jax.random.randint(own_keys[2], (C,), 0, R + 1), jax.random.fold_in(own_keys[2], 1), 0, R).astype(jnp.int32),
    }


eps = 1e-06

def dft_table():
    times = jnp.arange(S, dtype=jnp.int32)
    bins = 1 + jnp.arange(F + 2 * HALF_SMOOTH, dtype=jnp.int32)
    phase = times[:, None] * bins[None, :] % S
    angle = 2.0 * math.pi / S * phase.astype(jnp.float32)
    return jnp.concatenate([jnp.cos(angle), -jnp.sin(angle)], axis=1).astype(jnp.bfloat16)

def smoothing_table():
    inner = jnp.arange(F + 2 * HALF_SMOOTH, dtype=jnp.int32)[:, None]
    outer = jnp.arange(F, dtype=jnp.int32)[None, :]
    return ((inner >= outer) & (inner <= outer + 2 * HALF_SMOOTH)).astype(jnp.float32)

def lag_table():
    bins = 1 + HALF_SMOOTH + jnp.arange(F, dtype=jnp.int32)
    shifts = jnp.arange(2 * LARGEST_LAG_SPAN + 1, dtype=jnp.int32) - LARGEST_LAG_SPAN
    phase = bins[:, None] * shifts[None, :] % S
    angle = 2.0 * math.pi / S * phase.astype(jnp.float32)
    return jnp.concatenate([jnp.cos(angle), -jnp.sin(angle)], axis=0).astype(jnp.bfloat16)

def whiten_masked(masked):
    count, window_segments, samples = masked.shape
    spectra = jnp.dot(masked.reshape(count * window_segments, samples), dft_table(), preferred_element_type=jnp.float32)
    half = spectra.shape[1] // 2
    real_component = spectra[:, :half]
    imag_part = spectra[:, half:]
    amplitude = jnp.sqrt(real_component * real_component + imag_part * imag_part)
    smooth = jnp.dot(amplitude, smoothing_table(), precision=lax.Precision.HIGHEST) / (2 * HALF_SMOOTH + 1)
    scale = 1.0 / (smooth + eps)
    core = jnp.concatenate([real_component[:, HALF_SMOOTH:HALF_SMOOTH + F] * scale, imag_part[:, HALF_SMOOTH:HALF_SMOOTH + F] * scale], axis=1)
    return core.astype(jnp.bfloat16).reshape(count, window_segments, 2 * F)

def diagonals(launch_lattice):
    blocks, rows, cols = launch_lattice.shape
    flat = launch_lattice.reshape(blocks, rows * cols)
    flat = jnp.concatenate([flat, jnp.zeros((blocks, rows), jnp.float32)], axis=1)
    return flat.reshape(blocks, rows, cols + 1)[:, :, :R + 1]

def correlate(local, extended, reach_part):
    chans, window_segments, _ = local.shape
    span = extended.shape[0]
    lag_all = lag_table()

    def one_block(total, index):
        start = index * FREQ_BLOCK

        def take(array, offset):
            return lax.dynamic_slice_in_dim(array, offset + start, FREQ_BLOCK, 2)
        left_spectra = jnp.concatenate([take(local, 0), take(local, F)], axis=1)
        ext_real = take(extended, 0)
        ext_imag = take(extended, F)
        right_spectra = jnp.concatenate([jnp.concatenate([ext_real, ext_imag], axis=1), jnp.concatenate([-ext_imag, ext_real], axis=1)], axis=0)
        launch_lattice = jnp.einsum('est,ust->teu', left_spectra.astype(jnp.float32), right_spectra.astype(jnp.float32)) / window_segments
        cross = jnp.concatenate([diagonals(launch_lattice[:, :, :span]), diagonals(launch_lattice[:, :, span:])], axis=0).astype(jnp.bfloat16)
        rows = jnp.concatenate([lax.dynamic_slice_in_dim(lag_all, start, FREQ_BLOCK, 0), lax.dynamic_slice_in_dim(lag_all, F + start, FREQ_BLOCK, 0)], axis=0)
        return (total + jnp.einsum('fck,fl->ckl', cross.astype(jnp.float32), rows.astype(jnp.float32)), None)
    starting_carry = jnp.zeros((chans, R + 1, 2 * LARGEST_LAG_SPAN + 1), jnp.float32)
    total, _ = lax.scan(one_block, starting_carry, jnp.arange(F // FREQ_BLOCK, dtype=jnp.int32))
    offsets = jnp.arange(R + 1, dtype=jnp.int32)
    keep = offsets[None, :] <= reach_part[:, None]
    return jnp.where(keep[:, :, None], total / math.sqrt(F), 0.0).astype(jnp.bfloat16)

def reference(traces, quality, reach):
    masked = traces * quality[:, :, None].astype(jnp.bfloat16)
    groups = C // CH_DEV
    whitened = lax.map(whiten_masked, masked.reshape(groups, CH_DEV, W, S)).reshape(C, W, 2 * F)
    padded = jnp.concatenate([whitened, jnp.zeros((R, W, 2 * F), jnp.bfloat16)], axis=0)

    def one_group(index):
        first = (index * CH_DEV).astype(jnp.int32)
        local = lax.dynamic_slice_in_dim(whitened, first, CH_DEV, 0)
        extended = lax.dynamic_slice_in_dim(padded, first, CH_DEV + R, 0)
        reach_part = lax.dynamic_slice_in_dim(reach, first, CH_DEV, 0)
        return correlate(local, extended, reach_part)
    result = lax.map(one_group, jnp.arange(groups, dtype=jnp.int32))
    return result.reshape(C, R + 1, 2 * LARGEST_LAG_SPAN + 1)
```

```python
import math

import jax
import jax.numpy as jnp
import numpy as np
from jax import lax
from jax.experimental import pallas as pl
from jax.experimental.pallas import tpu as pltpu
from jax.sharding import PartitionSpec as P

R = 160
S = 1500
F = 256
HALF_SMOOTH = 32
BINS = F + 2 * HALF_SMOOTH
LAG = 100
LAGS = 2 * LAG + 1
LANES = 128
PIECES = -(-S // LANES)
GROUP = 8
GROUPS = F // GROUP
BAND = 176
SPAN = 256
STEP_GROUPS = 4
STEP_CHANS = 8
VMEM_LIMIT = 56 * 1024 * 1024

eps = 1e-06


def dft_rows():
    times = np.arange(S, dtype=np.int32)
    bins = 1 + np.arange(BINS, dtype=np.int32)
    phase = bins[:, None] * times[None, :] % S
    angle = np.float32(2.0 * math.pi / S) * phase.astype(np.float32)
    table = np.concatenate([np.cos(angle), -np.sin(angle)], axis=0)
    return np.pad(table, ((0, 0), (0, PIECES * LANES - S))).astype(jnp.bfloat16)


def band_rows():
    outer = np.arange(F)[:, None]
    inner = np.arange(BINS)[None, :]
    return ((inner >= outer) & (inner <= outer + 2 * HALF_SMOOTH)).astype(jnp.bfloat16)


def lag_rows(windows):
    bins = 1 + HALF_SMOOTH + np.arange(F, dtype=np.int32)
    shifts = np.arange(LAGS, dtype=np.int32) - LAG
    phase = shifts[:, None] * bins[None, :] % S
    angle = np.float32(2.0 * math.pi / S) * phase.astype(np.float32)
    both = np.stack([np.cos(angle), -np.sin(angle)], axis=1).astype(jnp.bfloat16)
    both = both.reshape(LAGS, 2, GROUPS, GROUP).transpose(0, 2, 1, 3).reshape(LAGS, 2 * F)
    scale = np.float32(1.0 / (windows * math.sqrt(F)))
    both = (both.astype(np.float32) * scale).astype(jnp.bfloat16)
    return np.concatenate([both, np.zeros((256 - LAGS, 2 * F), jnp.bfloat16)], axis=0)


def whiten_kernel(traces_ref, quality_ref, dft_ref, band_ref, out_ref, wide, turned):
    chans, windows, _ = traces_ref.shape
    pieces = wide.shape[0]
    for c in range(0, chans, 8):
        rows = traces_ref[c : c + 8].astype(jnp.float32).reshape(8 * windows, S)
        for p in range(pieces):
            piece = rows[:, p * LANES : (p + 1) * LANES]
            if piece.shape[1] < LANES:
                rest = jnp.zeros((8 * windows, LANES - piece.shape[1]), jnp.float32)
                piece = jnp.concatenate([piece, rest], axis=1)
            wide[p, c * windows : (c + 8) * windows, :] = piece
    fill = jnp.zeros((LANES - chans, pieces * LANES), jnp.bfloat16)

    def window(w):
        rows = [wide[p, pl.ds(w, chans, stride=windows), :] for p in range(pieces)]
        return jnp.concatenate(rows, axis=1).astype(jnp.bfloat16)

    for w in range(0, windows, 2):
        both = jnp.concatenate([window(w), fill, window(w + 1), fill], axis=0)
        spectra = lax.dot_general(
            dft_ref[...], both, (((1,), (1,)), ((), ())), preferred_element_type=jnp.float32
        )
        real = spectra[:BINS]
        imag = spectra[BINS:]
        amplitude = jnp.sqrt(real * real + imag * imag)
        high = amplitude.astype(jnp.bfloat16)
        low = (amplitude - high.astype(jnp.float32)).astype(jnp.bfloat16)
        smooth = jnp.dot(band_ref[...], high, preferred_element_type=jnp.float32)
        smooth = smooth + jnp.dot(band_ref[...], low, preferred_element_type=jnp.float32)
        scale = 1.0 / (smooth * (1.0 / (2 * HALF_SMOOTH + 1)) + eps)
        usable = quality_ref[:, w * LANES : (w + 2) * LANES]
        scale = scale * usable
        real = real[HALF_SMOOTH : HALF_SMOOTH + F] * scale
        imag = imag[HALF_SMOOTH : HALF_SMOOTH + F] * scale
        for j in range(2):
            lanes = slice(j * LANES, (j + 1) * LANES)
            turned[:, 0, w + j] = real[:, lanes].reshape(GROUPS, GROUP, LANES)
            turned[:, 1, w + j] = imag[:, lanes].reshape(GROUPS, GROUP, LANES)
    depth = 2 * windows * GROUP
    for g in range(GROUPS):
        block = turned[g].reshape(depth, LANES).T
        out_ref[:, g * depth : (g + 1) * depth] = block[:chans].astype(jnp.bfloat16)


def whiten(traces, quality):
    chans, windows, _ = traces.shape
    usable = jnp.pad(quality.astype(jnp.float32).T, ((0, 0), (0, LANES - chans)))
    usable = usable.reshape(1, windows * LANES)
    depth = 2 * windows * GROUP
    return pl.pallas_call(
        whiten_kernel,
        out_shape=jax.ShapeDtypeStruct((chans, GROUPS * depth), jnp.bfloat16),
        in_specs=[pl.BlockSpec(memory_space=pltpu.VMEM)] * 4,
        out_specs=pl.BlockSpec(memory_space=pltpu.VMEM),
        scratch_shapes=[
            pltpu.VMEM((PIECES, chans * windows, LANES), jnp.float32),
            pltpu.VMEM((GROUPS, 2, windows, GROUP, LANES), jnp.float32),
        ],
        compiler_params=pltpu.CompilerParams(vmem_limit_bytes=VMEM_LIMIT),
        cost_estimate=pl.CostEstimate(
            flops=2 * chans * windows * S * 2 * BINS, bytes_accessed=8_000_000, transcendentals=0
        ),
    )(traces, usable, jnp.asarray(dft_rows()), jnp.asarray(band_rows()))


def correlate_kernel(
    gram_steps, reach_ref, own_ref, near_ref, far_odd_ref, far_even_ref, lag_ref, out_ref, cross, slab
):
    chans = own_ref.shape[0]
    depth = own_ref.shape[1] // STEP_GROUPS
    half = depth // 2
    step = pl.program_id(0)

    @pl.when(step < gram_steps)
    def _():
        spot = lax.broadcasted_iota(jnp.int32, (GROUP, half), 1) % GROUP
        row = lax.broadcasted_iota(jnp.int32, (GROUP, half), 0)
        mask = (spot == row)[None]
        for g in range(STEP_GROUPS):
            columns = slice(g * depth, (g + 1) * depth)
            own = own_ref[:, columns]
            far = far_odd_ref[:, columns] + far_even_ref[:, columns]
            fill = jnp.zeros((SPAN - 3 * chans, depth), jnp.bfloat16)
            others = jnp.concatenate([own, near_ref[:, columns], far, fill], axis=0)
            value = own.astype(jnp.float32)
            real = jnp.where(mask, value[:, None, :half], 0.0)
            imag = jnp.where(mask, value[:, None, half:], 0.0)
            left = jnp.concatenate(
                [
                    jnp.concatenate([real, imag], axis=2),
                    jnp.concatenate([imag, -real], axis=2),
                ],
                axis=1,
            ).astype(jnp.bfloat16)
            products = lax.dot_general(
                left.reshape(chans * 2 * GROUP, depth),
                others,
                (((1,), (1,)), ((), ())),
                preferred_element_type=jnp.float32,
            )
            start = pl.multiple_of((step * STEP_GROUPS + g) * 2 * GROUP, 2 * GROUP)
            cross[:, pl.ds(start, 2 * GROUP), :] = products.astype(jnp.bfloat16).reshape(
                chans, 2 * GROUP, SPAN
            )

    @pl.when(step >= gram_steps)
    def _():
        offsets = lax.broadcasted_iota(jnp.int32, (R + 1, LAGS), 0)
        base = pl.multiple_of((step - gram_steps) * STEP_CHANS, STEP_CHANS)
        for j in range(STEP_CHANS):
            c = base + j
            lagged = jnp.dot(lag_ref[...], cross[c], preferred_element_type=jnp.float32)
            slab[j] = lagged.T
            band = slab.at[j, pl.ds(base, BAND), :][j : j + R + 1, :LAGS]
            out_ref[j] = jnp.where(offsets <= reach_ref[c], band, 0.0).astype(jnp.bfloat16)


def correlate(windows, reach, own, near, far_odd, far_even):
    chans, columns = own.shape
    gram_steps = GROUPS // STEP_GROUPS
    block = pl.BlockSpec(
        (chans, columns // gram_steps), lambda i: (0, jnp.minimum(i, gram_steps - 1))
    )

    def kernel(*refs):
        correlate_kernel(gram_steps, *refs)

    return pl.pallas_call(
        kernel,
        grid=(gram_steps + chans // STEP_CHANS,),
        out_shape=jax.ShapeDtypeStruct((chans, R + 1, LAGS), jnp.bfloat16),
        in_specs=[pl.BlockSpec(memory_space=pltpu.SMEM)]
        + [block] * 4
        + [pl.BlockSpec(memory_space=pltpu.VMEM)],
        out_specs=pl.BlockSpec(
            (STEP_CHANS, R + 1, LAGS), lambda i: (jnp.maximum(i - gram_steps, 0), 0, 0)
        ),
        scratch_shapes=[
            pltpu.VMEM((chans, 2 * F, SPAN), jnp.bfloat16),
            pltpu.VMEM((STEP_CHANS, SPAN, 256), jnp.float32),
        ],
        compiler_params=pltpu.CompilerParams(vmem_limit_bytes=VMEM_LIMIT),
        cost_estimate=pl.CostEstimate(
            flops=20_000_000_000, bytes_accessed=12_000_000, transcendentals=0
        ),
    )(reach, own, near, far_odd, far_even, jnp.asarray(lag_rows(windows)))


def local(traces, quality, reach):
    windows = traces.shape[1]
    count = lax.axis_size("chan")
    own = whiten(traces, quality)
    near = lax.ppermute(own, "chan", [(i, i - 1) for i in range(1, count)])
    far_odd = lax.ppermute(own, "chan", [(i, i - 2) for i in range(3, count, 2)])
    far_even = lax.ppermute(near, "chan", [(i, i - 1) for i in range(1, count, 2)])
    return correlate(windows, reach, own, near, far_odd, far_even)


def solution(mesh):
    return jax.shard_map(
        local,
        mesh=mesh,
        in_specs=(P(("day", "chan"), None, None), P(("day", "chan"), None), P(("day", "chan"))),
        out_specs=P(("day", "chan"), None, None),
        check_vma=False,
    )
```

```python
import math

import jax
import jax.numpy as jnp
import numpy as np
from jax import lax
from jax.experimental import pallas as pl
from jax.experimental.pallas import tpu as pltpu
from jax.sharding import PartitionSpec as P

R = 160
S = 1500
F = 256
HALF_SMOOTH = 32
BINS = F + 2 * HALF_SMOOTH
LAG = 100
LAGS = 2 * LAG + 1
LANES = 128
PIECES = -(-S // LANES)
GROUP = 8
GROUPS = F // GROUP
SPAN = 256
STEP_GROUPS = 4
STEP_CHANS = 16
COLUMNS = 1024
EARLY = 16
VMEM_LIMIT = 56 * 1024 * 1024

eps = 1e-06


def dft_rows():
    times = np.arange(S, dtype=np.int32)
    bins = 1 + np.arange(BINS, dtype=np.int32)
    phase = bins[:, None] * times[None, :] % S
    angle = np.float32(2.0 * math.pi / S) * phase.astype(np.float32)
    table = np.concatenate([np.cos(angle), -np.sin(angle)], axis=0)
    return np.pad(table, ((0, 0), (0, PIECES * LANES - S))).astype(jnp.bfloat16)


def band_rows():
    outer = np.arange(F)[:, None]
    inner = np.arange(BINS)[None, :]
    return ((inner >= outer) & (inner <= outer + 2 * HALF_SMOOTH)).astype(jnp.bfloat16)


def lag_rows(windows):
    bins = 1 + HALF_SMOOTH + np.arange(F, dtype=np.int32)
    shifts = np.arange(LAGS, dtype=np.int32) - LAG
    phase = shifts[:, None] * bins[None, :] % S
    angle = np.float32(2.0 * math.pi / S) * phase.astype(np.float32)
    both = np.stack([np.cos(angle), -np.sin(angle)], axis=1).astype(jnp.bfloat16)
    both = both.reshape(LAGS, 2, GROUPS, GROUP).transpose(0, 2, 1, 3).reshape(LAGS, 2 * F)
    scale = np.float32(1.0 / (windows * math.sqrt(F)))
    both = (both.astype(np.float32) * scale).astype(jnp.bfloat16)
    return np.concatenate([both, np.zeros((256 - LAGS, 2 * F), jnp.bfloat16)], axis=0)


def whiten_kernel(traces_ref, quality_ref, dft_ref, band_ref, first_ref, second_ref, wide, turned):
    chans, windows, _ = traces_ref.shape
    pieces = wide.shape[0]
    for c in range(0, chans, 8):
        rows = traces_ref[c : c + 8].astype(jnp.float32).reshape(8 * windows, S)
        for p in range(pieces):
            piece = rows[:, p * LANES : (p + 1) * LANES]
            if piece.shape[1] < LANES:
                rest = jnp.zeros((8 * windows, LANES - piece.shape[1]), jnp.float32)
                piece = jnp.concatenate([piece, rest], axis=1)
            wide[p, c * windows : (c + 8) * windows, :] = piece
    fill = jnp.zeros((LANES - chans, pieces * LANES), jnp.bfloat16)

    def window(w):
        rows = [wide[p, pl.ds(w, chans, stride=windows), :] for p in range(pieces)]
        return jnp.concatenate(rows, axis=1).astype(jnp.bfloat16)

    for w in range(0, windows, 2):
        both = jnp.concatenate([window(w), fill, window(w + 1), fill], axis=0)
        spectra = lax.dot_general(
            dft_ref[...], both, (((1,), (1,)), ((), ())), preferred_element_type=jnp.float32
        )
        real = spectra[:BINS]
        imag = spectra[BINS:]
        amplitude = jnp.sqrt(real * real + imag * imag)
        high = amplitude.astype(jnp.bfloat16)
        low = (amplitude - high.astype(jnp.float32)).astype(jnp.bfloat16)
        smooth = jnp.dot(band_ref[...], high, preferred_element_type=jnp.float32)
        smooth = smooth + jnp.dot(band_ref[...], low, preferred_element_type=jnp.float32)
        scale = 1.0 / (smooth * (1.0 / (2 * HALF_SMOOTH + 1)) + eps)
        usable = quality_ref[:, w * LANES : (w + 2) * LANES]
        scale = scale * usable
        real = real[HALF_SMOOTH : HALF_SMOOTH + F] * scale
        imag = imag[HALF_SMOOTH : HALF_SMOOTH + F] * scale
        for j in range(2):
            lanes = slice(j * LANES, (j + 1) * LANES)
            turned[:, 0, w + j] = real[:, lanes].reshape(GROUPS, GROUP, LANES)
            turned[:, 1, w + j] = imag[:, lanes].reshape(GROUPS, GROUP, LANES)
    depth = 2 * windows * GROUP
    for g in range(GROUPS):
        block = turned[g].reshape(depth, LANES).T
        block = block[:chans].astype(jnp.bfloat16)
        if g < EARLY:
            first_ref[:, g * depth : (g + 1) * depth] = block
        else:
            second_ref[:, (g - EARLY) * depth : (g - EARLY + 1) * depth] = block


def whiten(traces, quality):
    chans, windows, _ = traces.shape
    usable = jnp.pad(quality.astype(jnp.float32).T, ((0, 0), (0, LANES - chans)))
    usable = usable.reshape(1, windows * LANES)
    depth = 2 * windows * GROUP
    return pl.pallas_call(
        whiten_kernel,
        out_shape=[
            jax.ShapeDtypeStruct((chans, EARLY * depth), jnp.bfloat16),
            jax.ShapeDtypeStruct((chans, (GROUPS - EARLY) * depth), jnp.bfloat16),
        ],
        in_specs=[pl.BlockSpec(memory_space=pltpu.VMEM)] * 4,
        out_specs=[pl.BlockSpec(memory_space=pltpu.VMEM)] * 2,
        scratch_shapes=[
            pltpu.VMEM((PIECES, chans * windows, LANES), jnp.float32),
            pltpu.VMEM((GROUPS, 2, windows, GROUP, LANES), jnp.float32),
        ],
        compiler_params=pltpu.CompilerParams(vmem_limit_bytes=VMEM_LIMIT),
        cost_estimate=pl.CostEstimate(
            flops=2 * chans * windows * S * 2 * BINS, bytes_accessed=8_000_000, transcendentals=0
        ),
    )(traces, usable, jnp.asarray(dft_rows()), jnp.asarray(band_rows()))


def gram(own_ref, near_ref, far_odd_ref, far_even_ref, store):
    chans = own_ref.shape[0]
    depth = own_ref.shape[1] // STEP_GROUPS
    half = depth // 2
    spot = lax.broadcasted_iota(jnp.int32, (GROUP, half), 1) % GROUP
    row = lax.broadcasted_iota(jnp.int32, (GROUP, half), 0)
    mask = (spot == row)[None]
    for g in range(STEP_GROUPS):
        columns = slice(g * depth, (g + 1) * depth)
        own = own_ref[:, columns]
        far = far_odd_ref[:, columns] + far_even_ref[:, columns]
        fill = jnp.zeros((SPAN - 3 * chans, depth), jnp.bfloat16)
        others = jnp.concatenate([own, near_ref[:, columns], far, fill], axis=0)
        value = own.astype(jnp.float32)
        real = jnp.where(mask, value[:, None, :half], 0.0)
        imag = jnp.where(mask, value[:, None, half:], 0.0)
        left = jnp.concatenate(
            [
                jnp.concatenate([real, imag], axis=2),
                jnp.concatenate([imag, -real], axis=2),
            ],
            axis=1,
        ).astype(jnp.bfloat16)
        products = lax.dot_general(
            left.reshape(chans * 2 * GROUP, depth),
            others,
            (((1,), (1,)), ((), ())),
            preferred_element_type=jnp.float32,
        )
        store(g, products.astype(jnp.bfloat16).reshape(chans, 2 * GROUP, SPAN))


def early_kernel(own_ref, near_ref, far_odd_ref, far_even_ref, cross_ref):
    def store(g, products):
        cross_ref[:, g * 2 * GROUP : (g + 1) * 2 * GROUP, :] = products

    gram(own_ref, near_ref, far_odd_ref, far_even_ref, store)


def early_cross(own, near, far_odd, far_even):
    chans, columns = own.shape
    steps = columns // COLUMNS
    block = pl.BlockSpec((chans, COLUMNS), lambda i: (0, i))
    rows = STEP_GROUPS * 2 * GROUP
    return pl.pallas_call(
        early_kernel,
        grid=(steps,),
        out_shape=jax.ShapeDtypeStruct((chans, steps * rows, SPAN), jnp.bfloat16),
        in_specs=[block] * 4,
        out_specs=pl.BlockSpec((chans, rows, SPAN), lambda i: (0, i, 0)),
        compiler_params=pltpu.CompilerParams(vmem_limit_bytes=VMEM_LIMIT),
        cost_estimate=pl.CostEstimate(
            flops=8_000_000_000, bytes_accessed=13_000_000, transcendentals=0
        ),
    )(own, near, far_odd, far_even)


def late_kernel(
    gram_steps,
    reach_ref,
    own_ref,
    near_ref,
    far_odd_ref,
    far_even_ref,
    early_ref,
    lag_ref,
    out_ref,
    cross,
    turned,
):
    chans = own_ref.shape[0]
    step = pl.program_id(0)

    @pl.when(step < gram_steps)
    def _():
        def store(g, products):
            start = pl.multiple_of((step * STEP_GROUPS + g) * 2 * GROUP, 2 * GROUP)
            cross[:, pl.ds(start, 2 * GROUP), :] = products

        gram(own_ref, near_ref, far_odd_ref, far_even_ref, store)

    @pl.when(step >= gram_steps)
    def _():
        depth = early_ref.shape[1]
        base = (step - gram_steps) * STEP_CHANS
        for j in range(STEP_CHANS):
            c = base + j
            lagged = jnp.dot(lag_ref[:, :depth], early_ref[j], preferred_element_type=jnp.float32)
            lagged = lagged + jnp.dot(
                lag_ref[:, depth:], cross[c], preferred_element_type=jnp.float32
            )
            start = (chans - c) * STEP_CHANS + j
            for p in range(2):
                part = lagged[p * LANES : (p + 1) * LANES].T
                turned[p, pl.ds(start, SPAN, stride=STEP_CHANS), :] = part
        first = chans * STEP_CHANS
        last = first + (R + 1) * STEP_CHANS
        offsets = lax.broadcasted_iota(jnp.int32, (R + 1, STEP_CHANS, LANES), 0)
        keep = offsets <= reach_ref[...][None]
        for p in range(2):
            width = min(LANES, LAGS - p * LANES)
            part = turned[p, first:last, :].reshape(R + 1, STEP_CHANS, LANES)
            part = jnp.where(keep, part, 0.0).astype(jnp.bfloat16)
            out_ref[:, :, p * LANES : p * LANES + width] = part[:, :, :width]


def late_correlate(windows, reach, own, near, far_odd, far_even, early):
    chans, columns = own.shape
    gram_steps = columns // COLUMNS
    depth = early.shape[1]
    block = pl.BlockSpec((chans, COLUMNS), lambda i: (0, jnp.minimum(i, gram_steps - 1)))

    def later(i):
        return jnp.maximum(i - gram_steps, 0)

    def kernel(*refs):
        late_kernel(gram_steps, *refs)

    turned = pl.pallas_call(
        kernel,
        grid=(gram_steps + chans // STEP_CHANS,),
        out_shape=jax.ShapeDtypeStruct((R + 1, chans, LAGS), jnp.bfloat16),
        in_specs=[pl.BlockSpec((STEP_CHANS, LANES), lambda i: (later(i), 0))]
        + [block] * 4
        + [pl.BlockSpec((STEP_CHANS, depth, SPAN), lambda i: (later(i), 0, 0))]
        + [pl.BlockSpec(memory_space=pltpu.VMEM)],
        out_specs=pl.BlockSpec((R + 1, STEP_CHANS, LAGS), lambda i: (0, later(i), 0)),
        scratch_shapes=[
            pltpu.VMEM((chans, 2 * F - depth, SPAN), jnp.bfloat16),
            pltpu.VMEM((2, (chans + SPAN) * STEP_CHANS, LANES), jnp.float32),
        ],
        compiler_params=pltpu.CompilerParams(vmem_limit_bytes=VMEM_LIMIT),
        cost_estimate=pl.CostEstimate(
            flops=12_000_000_000, bytes_accessed=20_000_000, transcendentals=0
        ),
    )(
        jnp.broadcast_to(reach[:, None], (chans, LANES)),
        own,
        near,
        far_odd,
        far_even,
        early,
        jnp.asarray(lag_rows(windows)),
    )
    return jnp.transpose(turned, (1, 0, 2))


def follow_kernel(value_ref, near_ref, far_ref, out_ref):
    pass


def follow(value, near, far):
    return pl.pallas_call(
        follow_kernel,
        out_shape=jax.ShapeDtypeStruct(value.shape, value.dtype),
        in_specs=[pl.BlockSpec(memory_space=pl.ANY)] * 3,
        out_specs=pl.BlockSpec(memory_space=pl.ANY),
        input_output_aliases={0: 0},
    )(value, near, far)


def neighbours(own):
    count = lax.axis_size("chan")
    near = lax.ppermute(own, "chan", [(i, i - 1) for i in range(1, count)])
    far_odd = lax.ppermute(own, "chan", [(i, i - 2) for i in range(3, count, 2)])
    return near, far_odd


def relayed(near):
    count = lax.axis_size("chan")
    return lax.ppermute(near, "chan", [(i, i - 1) for i in range(1, count, 2)])


def local(traces, quality, reach):
    windows = traces.shape[1]
    first, second = whiten(traces, quality)
    near, far_odd = neighbours(first)
    second = follow(second, near, far_odd)
    early = early_cross(first, near, far_odd, relayed(near))
    near, far_odd = neighbours(second)
    near = follow(near, early, early)
    return late_correlate(windows, reach, second, near, far_odd, relayed(near), early)


def solution(mesh):
    return jax.shard_map(
        local,
        mesh=mesh,
        in_specs=(P(("day", "chan"), None, None), P(("day", "chan"), None), P(("day", "chan"))),
        out_specs=P(("day", "chan"), None, None),
        check_vma=False,
    )
```

```python
import math

import jax
import jax.numpy as jnp
import numpy as np
from jax import lax
from jax.experimental import pallas as pl
from jax.experimental.pallas import tpu as pltpu
from jax.sharding import PartitionSpec as P

R = 160
S = 1500
F = 256
HALF_SMOOTH = 32
BINS = F + 2 * HALF_SMOOTH
LAG = 100
LAGS = 2 * LAG + 1
LANES = 128
PIECES = -(-S // LANES)
GROUP = 8
GROUPS = F // GROUP
SPAN = 256
STEP_GROUPS = 4
STEP_CHANS = 16
PITCH = STEP_CHANS + 1
COLUMNS = 1024
EARLY = 16
VMEM_LIMIT = 56 * 1024 * 1024

eps = 1e-06


def dft_rows(first, last):
    times = np.arange(S, dtype=np.int32)
    bins = 1 + np.arange(first, last + 2 * HALF_SMOOTH, dtype=np.int32)
    phase = bins[:, None] * times[None, :] % S
    angle = np.float32(2.0 * math.pi / S) * phase.astype(np.float32)
    table = np.concatenate([np.cos(angle), -np.sin(angle)], axis=0)
    return np.pad(table, ((0, 0), (0, PIECES * LANES - S))).astype(jnp.bfloat16)


def band_rows(count):
    outer = np.arange(count)[:, None]
    inner = np.arange(count + 2 * HALF_SMOOTH)[None, :]
    return ((inner >= outer) & (inner <= outer + 2 * HALF_SMOOTH)).astype(jnp.bfloat16)


def lag_rows(windows):
    bins = 1 + HALF_SMOOTH + np.arange(F, dtype=np.int32)
    shifts = np.arange(LAGS, dtype=np.int32) - LAG
    phase = shifts[:, None] * bins[None, :] % S
    angle = np.float32(2.0 * math.pi / S) * phase.astype(np.float32)
    both = np.stack([np.cos(angle), -np.sin(angle)], axis=1).astype(jnp.bfloat16)
    both = both.reshape(LAGS, 2, GROUPS, GROUP).transpose(0, 2, 1, 3).reshape(LAGS, 2 * F)
    scale = np.float32(1.0 / (windows * math.sqrt(F)))
    both = (both.astype(np.float32) * scale).astype(jnp.bfloat16)
    return np.concatenate([both, np.zeros((256 - LAGS, 2 * F), jnp.bfloat16)], axis=0)


def arrange(traces_ref, rows_ref, wide):
    chans, windows, _ = traces_ref.shape
    pieces = wide.shape[0]
    pitch = windows + 1
    for c in range(chans):
        rows = traces_ref[c].astype(jnp.float32)
        for p in range(pieces):
            piece = rows[:, p * LANES : (p + 1) * LANES]
            if piece.shape[1] < LANES:
                rest = jnp.zeros((windows, LANES - piece.shape[1]), jnp.float32)
                piece = jnp.concatenate([piece, rest], axis=1)
            wide[p, c * pitch : c * pitch + windows, :] = piece
    for w in range(windows):
        for p in range(pieces):
            piece = wide[p, pl.ds(w, chans, stride=pitch), :]
            rows_ref[w, :, p * LANES : (p + 1) * LANES] = piece.astype(jnp.bfloat16)


def whiten_rows(rows_ref, quality_ref, dft_ref, band_ref, out_ref, turned):
    windows, chans, samples = rows_ref.shape
    count, bins = band_ref.shape
    fill = jnp.zeros((LANES - chans, samples), jnp.bfloat16)
    for w in range(0, windows, 2):
        both = jnp.concatenate([rows_ref[w], fill, rows_ref[w + 1], fill], axis=0)
        spectra = lax.dot_general(
            dft_ref[...], both, (((1,), (1,)), ((), ())), preferred_element_type=jnp.float32
        )
        real = spectra[:bins]
        imag = spectra[bins:]
        amplitude = jnp.sqrt(real * real + imag * imag)
        high = amplitude.astype(jnp.bfloat16)
        low = (amplitude - high.astype(jnp.float32)).astype(jnp.bfloat16)
        smooth = jnp.dot(band_ref[...], high, preferred_element_type=jnp.float32)
        smooth = smooth + jnp.dot(band_ref[...], low, preferred_element_type=jnp.float32)
        scale = 1.0 / (smooth * (1.0 / (2 * HALF_SMOOTH + 1)) + eps)
        usable = quality_ref[:, w * LANES : (w + 2) * LANES]
        scale = scale * usable
        real = real[HALF_SMOOTH : HALF_SMOOTH + count] * scale
        imag = imag[HALF_SMOOTH : HALF_SMOOTH + count] * scale
        for j in range(2):
            lanes = slice(j * LANES, (j + 1) * LANES)
            turned[:, 0, w + j] = real[:, lanes].reshape(count // GROUP, GROUP, LANES)
            turned[:, 1, w + j] = imag[:, lanes].reshape(count // GROUP, GROUP, LANES)
    depth = 2 * windows * GROUP
    for g in range(count // GROUP):
        block = turned[g].reshape(depth, LANES).T
        out_ref[:, g * depth : (g + 1) * depth] = block[:chans].astype(jnp.bfloat16)


def first_kernel(traces_ref, quality_ref, dft_ref, band_ref, out_ref, rows_ref, turned, wide):
    arrange(traces_ref, rows_ref, wide)
    whiten_rows(rows_ref, quality_ref, dft_ref, band_ref, out_ref, turned)


def whiten(source, usable, first, last, arranged):
    windows = usable.shape[1] // LANES
    chans = source.shape[1] if arranged else source.shape[0]
    groups = (last - first) // GROUP
    bins = last - first + 2 * HALF_SMOOTH
    depth = 2 * windows * GROUP
    whole = pl.BlockSpec(memory_space=pltpu.VMEM)
    out = [jax.ShapeDtypeStruct((chans, groups * depth), jnp.bfloat16)]
    scratch = [pltpu.VMEM((groups, 2, windows, GROUP, LANES), jnp.float32)]
    if not arranged:
        out.append(jax.ShapeDtypeStruct((windows, chans, PIECES * LANES), jnp.bfloat16))
        scratch.append(pltpu.VMEM((PIECES, chans * (windows + 1), LANES), jnp.float32))
    return pl.pallas_call(
        whiten_rows if arranged else first_kernel,
        out_shape=out,
        in_specs=[whole] * 4,
        out_specs=[whole] * len(out),
        scratch_shapes=scratch,
        compiler_params=pltpu.CompilerParams(vmem_limit_bytes=VMEM_LIMIT),
        cost_estimate=pl.CostEstimate(
            flops=4 * chans * windows * S * bins, bytes_accessed=8_000_000, transcendentals=0
        ),
    )(source, usable, jnp.asarray(dft_rows(first, last)), jnp.asarray(band_rows(last - first)))


def gram(own_ref, near_ref, far_odd_ref, far_even_ref, store):
    chans = own_ref.shape[0]
    depth = own_ref.shape[1] // STEP_GROUPS
    half = depth // 2
    spot = lax.broadcasted_iota(jnp.int32, (GROUP, half), 1) % GROUP
    row = lax.broadcasted_iota(jnp.int32, (GROUP, half), 0)
    mask = (spot == row)[None]
    for g in range(STEP_GROUPS):
        columns = slice(g * depth, (g + 1) * depth)
        own = own_ref[:, columns]
        far = far_odd_ref[:, columns] + far_even_ref[:, columns]
        fill = jnp.zeros((SPAN - 3 * chans, depth), jnp.bfloat16)
        others = jnp.concatenate([own, near_ref[:, columns], far, fill], axis=0)
        value = own.astype(jnp.float32)
        real = jnp.where(mask, value[:, None, :half], 0.0)
        imag = jnp.where(mask, value[:, None, half:], 0.0)
        left = jnp.concatenate(
            [
                jnp.concatenate([real, imag], axis=2),
                jnp.concatenate([imag, -real], axis=2),
            ],
            axis=1,
        ).astype(jnp.bfloat16)
        products = lax.dot_general(
            left.reshape(chans * 2 * GROUP, depth),
            others,
            (((1,), (1,)), ((), ())),
            preferred_element_type=jnp.float32,
        )
        store(g, products.astype(jnp.bfloat16).reshape(chans, 2 * GROUP, SPAN))


def early_kernel(own_ref, near_ref, far_odd_ref, far_even_ref, cross_ref):
    def store(g, products):
        cross_ref[:, g * 2 * GROUP : (g + 1) * 2 * GROUP, :] = products

    gram(own_ref, near_ref, far_odd_ref, far_even_ref, store)


def early_cross(own, near, far_odd, far_even):
    chans, columns = own.shape
    steps = columns // COLUMNS
    block = pl.BlockSpec((chans, COLUMNS), lambda i: (0, i))
    rows = STEP_GROUPS * 2 * GROUP
    return pl.pallas_call(
        early_kernel,
        grid=(steps,),
        out_shape=jax.ShapeDtypeStruct((chans, steps * rows, SPAN), jnp.bfloat16),
        in_specs=[block] * 4,
        out_specs=pl.BlockSpec((chans, rows, SPAN), lambda i: (0, i, 0)),
        compiler_params=pltpu.CompilerParams(vmem_limit_bytes=VMEM_LIMIT),
        cost_estimate=pl.CostEstimate(
            flops=8_000_000_000, bytes_accessed=13_000_000, transcendentals=0
        ),
    )(own, near, far_odd, far_even)


def late_kernel(
    gram_steps,
    reach_ref,
    own_ref,
    near_ref,
    far_odd_ref,
    far_even_ref,
    early_ref,
    lag_ref,
    out_ref,
    cross,
    turned,
):
    chans = own_ref.shape[0]
    step = pl.program_id(0)

    @pl.when(step < gram_steps)
    def _():
        def store(g, products):
            start = pl.multiple_of((step * STEP_GROUPS + g) * 2 * GROUP, 2 * GROUP)
            cross[:, pl.ds(start, 2 * GROUP), :] = products

        gram(own_ref, near_ref, far_odd_ref, far_even_ref, store)

    @pl.when(step >= gram_steps)
    def _():
        depth = early_ref.shape[1]
        base = (step - gram_steps) * STEP_CHANS
        for j in range(STEP_CHANS):
            c = base + j
            lagged = jnp.dot(lag_ref[:, :depth], early_ref[j], preferred_element_type=jnp.float32)
            lagged = lagged + jnp.dot(
                lag_ref[:, depth:], cross[c], preferred_element_type=jnp.float32
            )
            start = (chans - c) * PITCH + j
            for p in range(2):
                part = lagged[p * LANES : (p + 1) * LANES].T
                turned[p, pl.ds(start, SPAN, stride=PITCH), :] = part
        reach = reach_ref[...]
        for k in range(R + 1):
            start = (chans + k) * PITCH
            for p in range(2):
                width = min(LANES, LAGS - p * LANES)
                part = jnp.where(reach >= k, turned[p, start : start + STEP_CHANS, :], 0.0)
                out_ref[k, :, p * LANES : p * LANES + width] = part[:, :width].astype(jnp.bfloat16)


def late_correlate(windows, reach, own, near, far_odd, far_even, early):
    chans, columns = own.shape
    gram_steps = columns // COLUMNS
    depth = early.shape[1]
    block = pl.BlockSpec((chans, COLUMNS), lambda i: (0, jnp.minimum(i, gram_steps - 1)))

    def later(i):
        return jnp.maximum(i - gram_steps, 0)

    def kernel(*refs):
        late_kernel(gram_steps, *refs)

    turned = pl.pallas_call(
        kernel,
        grid=(gram_steps + chans // STEP_CHANS,),
        out_shape=jax.ShapeDtypeStruct((R + 1, chans, LAGS), jnp.bfloat16),
        in_specs=[pl.BlockSpec((STEP_CHANS, LANES), lambda i: (later(i), 0))]
        + [block] * 4
        + [pl.BlockSpec((STEP_CHANS, depth, SPAN), lambda i: (later(i), 0, 0))]
        + [pl.BlockSpec(memory_space=pltpu.VMEM)],
        out_specs=pl.BlockSpec((R + 1, STEP_CHANS, LAGS), lambda i: (0, later(i), 0)),
        scratch_shapes=[
            pltpu.VMEM((chans, 2 * F - depth, SPAN), jnp.bfloat16),
            pltpu.VMEM((2, (chans + SPAN) * PITCH, LANES), jnp.float32),
        ],
        compiler_params=pltpu.CompilerParams(vmem_limit_bytes=VMEM_LIMIT),
        cost_estimate=pl.CostEstimate(
            flops=12_000_000_000, bytes_accessed=20_000_000, transcendentals=0
        ),
    )(
        jnp.broadcast_to(reach[:, None], (chans, LANES)),
        own,
        near,
        far_odd,
        far_even,
        early,
        jnp.asarray(lag_rows(windows)),
    )
    return jnp.transpose(turned, (1, 0, 2))


def follow_kernel(value_ref, near_ref, far_ref, out_ref):
    pass


def follow(value, near, far):
    return pl.pallas_call(
        follow_kernel,
        out_shape=jax.ShapeDtypeStruct(value.shape, value.dtype),
        in_specs=[pl.BlockSpec(memory_space=pl.ANY)] * 3,
        out_specs=pl.BlockSpec(memory_space=pl.ANY),
        input_output_aliases={0: 0},
    )(value, near, far)


def neighbours(own):
    count = lax.axis_size("chan")
    near = lax.ppermute(own, "chan", [(i, i - 1) for i in range(1, count)])
    far_odd = lax.ppermute(own, "chan", [(i, i - 2) for i in range(3, count, 2)])
    return near, far_odd


def relayed(near):
    count = lax.axis_size("chan")
    return lax.ppermute(near, "chan", [(i, i - 1) for i in range(1, count, 2)])


def local(traces, quality, reach):
    windows = traces.shape[1]
    chans = traces.shape[0]
    usable = jnp.pad(quality.astype(jnp.float32).T, ((0, 0), (0, LANES - chans)))
    usable = usable.reshape(1, windows * LANES)
    split = EARLY * GROUP
    first, rows = whiten(traces, usable, 0, split, False)
    near, far_odd = neighbours(first)
    (second,) = whiten(rows, usable, split, F, True)
    next_near, next_odd = neighbours(second)
    near = follow(near, second, second)
    early = early_cross(first, near, far_odd, relayed(near))
    near = follow(next_near, early, early)
    return late_correlate(windows, reach, second, near, next_odd, relayed(near), early)


def solution(mesh):
    return jax.shard_map(
        local,
        mesh=mesh,
        in_specs=(P(("day", "chan"), None, None), P(("day", "chan"), None), P(("day", "chan"))),
        out_specs=P(("day", "chan"), None, None),
        check_vma=False,
    )
```

```python
import math

import jax
import jax.numpy as jnp
import numpy as np
from jax import lax
from jax.experimental import pallas as pl
from jax.experimental.pallas import tpu as pltpu
from jax.sharding import PartitionSpec as P

R = 160
S = 1500
F = 256
HALF_SMOOTH = 32
LAG = 100
LAGS = 2 * LAG + 1
LANES = 128
PIECES = -(-S // LANES)
GROUP = 8
GROUPS = F // GROUP
SPAN = 256
STEP_GROUPS = 4
STEP_CHANS = 16
PITCH = STEP_CHANS + 1
COLUMNS = 1024
WHITEN_CHANS = 16
VMEM_LIMIT = 56 * 1024 * 1024

eps = 1e-06


def dft_columns(first):
    times = np.arange(S, dtype=np.int32)
    own = first + HALF_SMOOTH + np.arange(LANES)
    sides = first + np.concatenate([np.arange(HALF_SMOOTH), LANES + HALF_SMOOTH + np.arange(HALF_SMOOTH)])

    def columns(bins):
        phase = times[:, None] * (1 + bins[None, :]).astype(np.int32) % S
        angle = np.float32(2.0 * math.pi / S) * phase.astype(np.float32)
        rest = ((0, PIECES * LANES - S), (0, LANES - bins.size))
        return [np.pad(part, rest) for part in (np.cos(angle), -np.sin(angle))]

    return np.concatenate(columns(own) + columns(sides), axis=1).astype(jnp.bfloat16)


def band_columns():
    rows = np.arange(LANES + 2 * HALF_SMOOTH)
    order = np.concatenate([rows[HALF_SMOOTH:-HALF_SMOOTH], rows[:HALF_SMOOTH], rows[-HALF_SMOOTH:]])
    outer = np.arange(LANES)[None, :]
    inside = (order[:, None] >= outer) & (order[:, None] <= outer + 2 * HALF_SMOOTH)
    return np.pad(inside, ((0, LANES - 2 * HALF_SMOOTH), (0, 0))).astype(jnp.bfloat16)


def lag_rows(windows):
    bins = 1 + HALF_SMOOTH + np.arange(F, dtype=np.int32)
    shifts = np.arange(LAGS, dtype=np.int32) - LAG
    phase = shifts[:, None] * bins[None, :] % S
    angle = np.float32(2.0 * math.pi / S) * phase.astype(np.float32)
    both = np.stack([np.cos(angle), -np.sin(angle)], axis=1).astype(jnp.bfloat16)
    both = both.reshape(LAGS, 2, GROUPS, GROUP).transpose(0, 2, 1, 3).reshape(LAGS, 2 * F)
    scale = np.float32(1.0 / (windows * math.sqrt(F)))
    both = (both.astype(np.float32) * scale).astype(jnp.bfloat16)
    return np.concatenate([both, np.zeros((256 - LAGS, 2 * F), jnp.bfloat16)], axis=0)


def whiten_kernel(traces_ref, quality_ref, dft_ref, band_ref, out_ref, wide):
    chans, windows, samples = traces_ref.shape
    pitch = windows + 1
    rows = traces_ref[...].reshape(chans * windows, samples)
    rest = jnp.zeros((chans * windows, PIECES * LANES - samples), jnp.bfloat16)
    rows = jnp.concatenate([rows, rest], axis=1)
    spectra = jnp.dot(rows, dft_ref[...], preferred_element_type=jnp.float32)
    own = [spectra[:, :LANES], spectra[:, LANES : 2 * LANES]]
    sides = [spectra[:, 2 * LANES : 3 * LANES], spectra[:, 3 * LANES :]]
    amplitude = jnp.concatenate(
        [jnp.sqrt(real * real + imag * imag) for real, imag in (own, sides)], axis=1
    )
    high = amplitude.astype(jnp.bfloat16)
    low = (amplitude - high.astype(jnp.float32)).astype(jnp.bfloat16)
    smooth = jnp.dot(high, band_ref[...], preferred_element_type=jnp.float32)
    smooth = smooth + jnp.dot(low, band_ref[...], preferred_element_type=jnp.float32)
    scale = quality_ref[...] / (smooth * (1.0 / (2 * HALF_SMOOTH + 1)) + eps)
    place = lax.broadcasted_iota(jnp.int32, (chans, LANES), 1) // GROUP
    for i in range(2):
        value = own[i] * scale
        for c in range(chans):
            wide[i, c * pitch : c * pitch + windows, :] = value[c * windows : (c + 1) * windows]
        turned = []
        for n in range(windows):
            w = (windows - n) % windows
            turned.append(pltpu.roll(wide[i, pl.ds(w, chans, stride=pitch), :], w * GROUP, 1))
        shift = 1
        while shift < windows:
            moves = (place // shift) % 2 == 1
            turned = [
                jnp.where(moves, turned[(n - shift) % windows], turned[n]) for n in range(windows)
            ]
            shift *= 2
        for g in range(windows):
            start = (2 * g + i) * LANES
            out_ref[:, start : start + LANES] = turned[g].astype(jnp.bfloat16)


def whiten(traces, usable, first):
    chans, windows, _ = traces.shape
    columns = 2 * LANES * windows
    whole = pl.BlockSpec(memory_space=pltpu.VMEM)
    return pl.pallas_call(
        whiten_kernel,
        grid=(chans // WHITEN_CHANS,),
        out_shape=jax.ShapeDtypeStruct((chans, columns), jnp.bfloat16),
        in_specs=[
            pl.BlockSpec((WHITEN_CHANS, windows, S), lambda i: (i, 0, 0)),
            pl.BlockSpec((WHITEN_CHANS * windows, LANES), lambda i: (i, 0)),
            whole,
            whole,
        ],
        out_specs=pl.BlockSpec((WHITEN_CHANS, columns), lambda i: (i, 0)),
        scratch_shapes=[pltpu.VMEM((2, WHITEN_CHANS * (windows + 1), LANES), jnp.float32)],
        compiler_params=pltpu.CompilerParams(vmem_limit_bytes=VMEM_LIMIT),
        cost_estimate=pl.CostEstimate(
            flops=8 * chans * windows * S * LANES, bytes_accessed=8_000_000, transcendentals=0
        ),
    )(traces, usable, jnp.asarray(dft_columns(first)), jnp.asarray(band_columns()))


def gram(own_ref, near_ref, far_odd_ref, far_even_ref, store):
    chans = own_ref.shape[0]
    depth = own_ref.shape[1] // STEP_GROUPS
    half = depth // 2
    spot = lax.broadcasted_iota(jnp.int32, (GROUP, half), 1) % GROUP
    row = lax.broadcasted_iota(jnp.int32, (GROUP, half), 0)
    mask = (spot == row)[None]
    for g in range(STEP_GROUPS):
        columns = slice(g * depth, (g + 1) * depth)
        own = own_ref[:, columns]
        far = far_odd_ref[:, columns] + far_even_ref[:, columns]
        fill = jnp.zeros((SPAN - 3 * chans, depth), jnp.bfloat16)
        others = jnp.concatenate([own, near_ref[:, columns], far, fill], axis=0)
        value = own.astype(jnp.float32)
        real = jnp.where(mask, value[:, None, :half], 0.0)
        imag = jnp.where(mask, value[:, None, half:], 0.0)
        left = jnp.concatenate(
            [
                jnp.concatenate([real, imag], axis=2),
                jnp.concatenate([imag, -real], axis=2),
            ],
            axis=1,
        ).astype(jnp.bfloat16)
        products = lax.dot_general(
            left.reshape(chans * 2 * GROUP, depth),
            others,
            (((1,), (1,)), ((), ())),
            preferred_element_type=jnp.float32,
        )
        store(g, products.astype(jnp.bfloat16).reshape(chans, 2 * GROUP, SPAN))


def early_kernel(own_ref, near_ref, far_odd_ref, far_even_ref, cross_ref):
    def store(g, products):
        cross_ref[:, g * 2 * GROUP : (g + 1) * 2 * GROUP, :] = products

    gram(own_ref, near_ref, far_odd_ref, far_even_ref, store)


def early_cross(own, near, far_odd, far_even):
    chans, columns = own.shape
    steps = columns // COLUMNS
    block = pl.BlockSpec((chans, COLUMNS), lambda i: (0, i))
    rows = STEP_GROUPS * 2 * GROUP
    return pl.pallas_call(
        early_kernel,
        grid=(steps,),
        out_shape=jax.ShapeDtypeStruct((chans, steps * rows, SPAN), jnp.bfloat16),
        in_specs=[block] * 4,
        out_specs=pl.BlockSpec((chans, rows, SPAN), lambda i: (0, i, 0)),
        compiler_params=pltpu.CompilerParams(vmem_limit_bytes=VMEM_LIMIT),
        cost_estimate=pl.CostEstimate(
            flops=8_000_000_000, bytes_accessed=13_000_000, transcendentals=0
        ),
    )(own, near, far_odd, far_even)


def late_kernel(
    gram_steps,
    reach_ref,
    own_ref,
    near_ref,
    far_odd_ref,
    far_even_ref,
    early_ref,
    lag_ref,
    out_ref,
    cross,
    turned,
):
    chans = own_ref.shape[0]
    step = pl.program_id(0)

    @pl.when(step < gram_steps)
    def _():
        def store(g, products):
            start = pl.multiple_of((step * STEP_GROUPS + g) * 2 * GROUP, 2 * GROUP)
            cross[:, pl.ds(start, 2 * GROUP), :] = products

        gram(own_ref, near_ref, far_odd_ref, far_even_ref, store)

    @pl.when(step >= gram_steps)
    def _():
        depth = early_ref.shape[1]
        base = (step - gram_steps) * STEP_CHANS
        for j in range(STEP_CHANS):
            c = base + j
            lagged = jnp.dot(lag_ref[:, :depth], early_ref[j], preferred_element_type=jnp.float32)
            lagged = lagged + jnp.dot(
                lag_ref[:, depth:], cross[c], preferred_element_type=jnp.float32
            )
            start = (chans - c) * PITCH + j
            for p in range(2):
                part = lagged[p * LANES : (p + 1) * LANES].T
                turned[p, pl.ds(start, SPAN, stride=PITCH), :] = part
        reach = reach_ref[...]
        for k in range(R + 1):
            start = (chans + k) * PITCH
            for p in range(2):
                width = min(LANES, LAGS - p * LANES)
                part = jnp.where(reach >= k, turned[p, start : start + STEP_CHANS, :], 0.0)
                out_ref[k, :, p * LANES : p * LANES + width] = part[:, :width].astype(jnp.bfloat16)


def late_correlate(windows, reach, own, near, far_odd, far_even, early):
    chans, columns = own.shape
    gram_steps = columns // COLUMNS
    depth = early.shape[1]
    block = pl.BlockSpec((chans, COLUMNS), lambda i: (0, jnp.minimum(i, gram_steps - 1)))

    def later(i):
        return jnp.maximum(i - gram_steps, 0)

    def kernel(*refs):
        late_kernel(gram_steps, *refs)

    turned = pl.pallas_call(
        kernel,
        grid=(gram_steps + chans // STEP_CHANS,),
        out_shape=jax.ShapeDtypeStruct((R + 1, chans, LAGS), jnp.bfloat16),
        in_specs=[pl.BlockSpec((STEP_CHANS, LANES), lambda i: (later(i), 0))]
        + [block] * 4
        + [pl.BlockSpec((STEP_CHANS, depth, SPAN), lambda i: (later(i), 0, 0))]
        + [pl.BlockSpec(memory_space=pltpu.VMEM)],
        out_specs=pl.BlockSpec((R + 1, STEP_CHANS, LAGS), lambda i: (0, later(i), 0)),
        scratch_shapes=[
            pltpu.VMEM((chans, 2 * F - depth, SPAN), jnp.bfloat16),
            pltpu.VMEM((2, (chans + SPAN) * PITCH, LANES), jnp.float32),
        ],
        compiler_params=pltpu.CompilerParams(vmem_limit_bytes=VMEM_LIMIT),
        cost_estimate=pl.CostEstimate(
            flops=12_000_000_000, bytes_accessed=20_000_000, transcendentals=0
        ),
    )(
        jnp.broadcast_to(reach[:, None], (chans, LANES)),
        own,
        near,
        far_odd,
        far_even,
        early,
        jnp.asarray(lag_rows(windows)),
    )
    return jnp.transpose(turned, (1, 0, 2))


def follow_kernel(value_ref, near_ref, far_ref, out_ref):
    pass


def follow(value, near, far):
    return pl.pallas_call(
        follow_kernel,
        out_shape=jax.ShapeDtypeStruct(value.shape, value.dtype),
        in_specs=[pl.BlockSpec(memory_space=pl.ANY)] * 3,
        out_specs=pl.BlockSpec(memory_space=pl.ANY),
        input_output_aliases={0: 0},
    )(value, near, far)


def neighbours(own):
    count = lax.axis_size("chan")
    near = lax.ppermute(own, "chan", [(i, i - 1) for i in range(1, count)])
    far_odd = lax.ppermute(own, "chan", [(i, i - 2) for i in range(3, count, 2)])
    return near, far_odd


def relayed(near):
    count = lax.axis_size("chan")
    return lax.ppermute(near, "chan", [(i, i - 1) for i in range(1, count, 2)])


def local(traces, quality, reach):
    windows = traces.shape[1]
    usable = quality.astype(jnp.float32).reshape(-1, 1)
    usable = jnp.broadcast_to(usable, (usable.shape[0], LANES))
    first = whiten(traces, usable, 0)
    near, far_odd = neighbours(first)
    second = whiten(traces, usable, LANES)
    next_near, next_odd = neighbours(second)
    near = follow(near, second, second)
    early = early_cross(first, near, far_odd, relayed(near))
    near = follow(next_near, early, early)
    return late_correlate(windows, reach, second, near, next_odd, relayed(near), early)


def solution(mesh):
    return jax.shard_map(
        local,
        mesh=mesh,
        in_specs=(P(("day", "chan"), None, None), P(("day", "chan"), None), P(("day", "chan"))),
        out_specs=P(("day", "chan"), None, None),
        check_vma=False,
    )
```

```python
import math

import jax
import jax.numpy as jnp
import numpy as np
from jax import lax
from jax.experimental import pallas as pl
from jax.experimental.pallas import tpu as pltpu
from jax.sharding import PartitionSpec as P

R = 160
S = 1500
F = 256
HALF_SMOOTH = 32
LAG = 100
LAGS = 2 * LAG + 1
LAG_ROWS = -(-LAGS // 16) * 16
LANES = 128
PIECES = -(-S // LANES)
GROUP = 8
GROUPS = F // GROUP
SPAN = 256
STEP_GROUPS = 4
STEP_CHANS = 16
PITCH = STEP_CHANS + 1
COLUMNS = 1024
WHITEN_CHANS = 16
VMEM_LIMIT = 56 * 1024 * 1024

eps = 1e-06


def dft_columns(first):
    times = np.arange(S, dtype=np.int32)
    own = first + HALF_SMOOTH + np.arange(LANES)
    sides = first + np.concatenate([np.arange(HALF_SMOOTH), LANES + HALF_SMOOTH + np.arange(HALF_SMOOTH)])

    def columns(bins):
        phase = times[:, None] * (1 + bins[None, :]).astype(np.int32) % S
        angle = np.float32(2.0 * math.pi / S) * phase.astype(np.float32)
        rest = ((0, PIECES * LANES - S), (0, LANES - bins.size))
        return [np.pad(part, rest) for part in (np.cos(angle), -np.sin(angle))]

    return np.concatenate(columns(own) + columns(sides), axis=1).astype(jnp.bfloat16)


def band_columns():
    rows = np.arange(LANES + 2 * HALF_SMOOTH)
    order = np.concatenate([rows[HALF_SMOOTH:-HALF_SMOOTH], rows[:HALF_SMOOTH], rows[-HALF_SMOOTH:]])
    outer = np.arange(LANES)[None, :]
    inside = (order[:, None] >= outer) & (order[:, None] <= outer + 2 * HALF_SMOOTH)
    return np.pad(inside, ((0, LANES - 2 * HALF_SMOOTH), (0, 0))).astype(jnp.bfloat16)


def lag_rows(windows):
    bins = 1 + HALF_SMOOTH + np.arange(F, dtype=np.int32)
    shifts = np.arange(LAGS, dtype=np.int32) - LAG
    phase = shifts[:, None] * bins[None, :] % S
    angle = np.float32(2.0 * math.pi / S) * phase.astype(np.float32)
    both = np.stack([np.cos(angle), -np.sin(angle)], axis=1).astype(jnp.bfloat16)
    both = both.reshape(LAGS, 2, GROUPS, GROUP).transpose(0, 2, 1, 3).reshape(LAGS, 2 * F)
    scale = np.float32(1.0 / (windows * math.sqrt(F)))
    both = (both.astype(np.float32) * scale).astype(jnp.bfloat16)
    return np.concatenate([both, np.zeros((LAG_ROWS - LAGS, 2 * F), jnp.bfloat16)], axis=0)


def whiten_kernel(traces_ref, quality_ref, dft_ref, band_ref, out_ref, wide):
    chans, windows, samples = traces_ref.shape
    pitch = windows + 1
    rows = traces_ref[...].reshape(chans * windows, samples)
    rest = jnp.zeros((chans * windows, PIECES * LANES - samples), jnp.bfloat16)
    rows = jnp.concatenate([rows, rest], axis=1)
    spectra = jnp.dot(rows, dft_ref[...], preferred_element_type=jnp.float32)
    own = [spectra[:, :LANES], spectra[:, LANES : 2 * LANES]]
    sides = [spectra[:, 2 * LANES : 3 * LANES], spectra[:, 3 * LANES :]]
    amplitude = jnp.concatenate(
        [jnp.sqrt(real * real + imag * imag) for real, imag in (own, sides)], axis=1
    )
    high = amplitude.astype(jnp.bfloat16)
    low = (amplitude - high.astype(jnp.float32)).astype(jnp.bfloat16)
    smooth = jnp.dot(high, band_ref[...], preferred_element_type=jnp.float32)
    smooth = smooth + jnp.dot(low, band_ref[...], preferred_element_type=jnp.float32)
    lane = lax.broadcasted_iota(jnp.int32, quality_ref.shape, 1) - pl.program_id(0) * chans
    quality = quality_ref[...].astype(jnp.float32)
    usable = [
        jnp.sum(jnp.where(lane == c, quality, 0.0), axis=1, keepdims=True) for c in range(chans)
    ]
    usable = jnp.concatenate([jnp.broadcast_to(u, (windows, LANES)) for u in usable], axis=0)
    scale = usable / (smooth * (1.0 / (2 * HALF_SMOOTH + 1)) + eps)
    place = lax.broadcasted_iota(jnp.int32, (chans, LANES), 1) // GROUP
    for i in range(2):
        value = own[i] * scale
        for c in range(chans):
            wide[i, c * pitch : c * pitch + windows, :] = value[c * windows : (c + 1) * windows]
        turned = []
        for n in range(windows):
            w = (windows - n) % windows
            turned.append(pltpu.roll(wide[i, pl.ds(w, chans, stride=pitch), :], w * GROUP, 1))
        shift = 1
        while shift < windows:
            moves = (place // shift) % 2 == 1
            turned = [
                jnp.where(moves, turned[(n - shift) % windows], turned[n]) for n in range(windows)
            ]
            shift *= 2
        for g in range(windows):
            start = (2 * g + i) * LANES
            out_ref[:, start : start + LANES] = turned[g].astype(jnp.bfloat16)


def whiten(traces, quality, first):
    chans, windows, _ = traces.shape
    columns = 2 * LANES * windows
    whole = pl.BlockSpec(memory_space=pltpu.VMEM)
    return pl.pallas_call(
        whiten_kernel,
        grid=(chans // WHITEN_CHANS,),
        out_shape=jax.ShapeDtypeStruct((chans, columns), jnp.bfloat16),
        in_specs=[
            pl.BlockSpec((WHITEN_CHANS, windows, S), lambda i: (i, 0, 0)),
            whole,
            whole,
            whole,
        ],
        out_specs=pl.BlockSpec((WHITEN_CHANS, columns), lambda i: (i, 0)),
        scratch_shapes=[pltpu.VMEM((2, WHITEN_CHANS * (windows + 1), LANES), jnp.float32)],
        compiler_params=pltpu.CompilerParams(vmem_limit_bytes=VMEM_LIMIT),
        cost_estimate=pl.CostEstimate(
            flops=8 * chans * windows * S * LANES, bytes_accessed=8_000_000, transcendentals=0
        ),
    )(traces, quality.T, jnp.asarray(dft_columns(first)), jnp.asarray(band_columns()))


def gram(own_ref, near_ref, far_odd_ref, far_even_ref, wide, store):
    chans = own_ref.shape[0]
    depth = own_ref.shape[1] // STEP_GROUPS
    half = depth // 2
    spot = lax.broadcasted_iota(jnp.int32, (GROUP, half), 1) % GROUP
    row = lax.broadcasted_iota(jnp.int32, (GROUP, half), 0)
    mask = spot == row
    for g in range(STEP_GROUPS):
        columns = slice(g * depth, (g + 1) * depth)
        own = own_ref[:, columns]
        far = far_odd_ref[:, columns] + far_even_ref[:, columns]
        fill = jnp.zeros((SPAN - 3 * chans, depth), jnp.bfloat16)
        others = jnp.concatenate([own, near_ref[:, columns], far, fill], axis=0)
        value = own.astype(jnp.float32)
        wide[2 * g] = value[:, :half]
        wide[2 * g + 1] = value[:, half:]
        left = []
        for c in range(chans):
            real = jnp.broadcast_to(wide[2 * g, c : c + 1, :], (GROUP, half))
            imag = jnp.broadcast_to(wide[2 * g + 1, c : c + 1, :], (GROUP, half))
            real = jnp.where(mask, real, 0.0)
            imag = jnp.where(mask, imag, 0.0)
            upper = jnp.concatenate([real, imag], axis=0).astype(jnp.bfloat16)
            lower = jnp.concatenate([imag, -real], axis=0).astype(jnp.bfloat16)
            left.append(jnp.concatenate([upper, lower], axis=1))
        products = lax.dot_general(
            jnp.concatenate(left, axis=0),
            others,
            (((1,), (1,)), ((), ())),
            preferred_element_type=jnp.float32,
        )
        store(g, products.astype(jnp.bfloat16).reshape(chans, 2 * GROUP, SPAN))


def early_kernel(own_ref, near_ref, far_odd_ref, far_even_ref, cross_ref, wide):
    def store(g, products):
        cross_ref[:, g * 2 * GROUP : (g + 1) * 2 * GROUP, :] = products

    gram(own_ref, near_ref, far_odd_ref, far_even_ref, wide, store)


def early_cross(own, near, far_odd, far_even):
    chans, columns = own.shape
    steps = columns // COLUMNS
    block = pl.BlockSpec((chans, COLUMNS), lambda i: (0, i))
    rows = STEP_GROUPS * 2 * GROUP
    return pl.pallas_call(
        early_kernel,
        grid=(steps,),
        out_shape=jax.ShapeDtypeStruct((chans, steps * rows, SPAN), jnp.bfloat16),
        in_specs=[block] * 4,
        out_specs=pl.BlockSpec((chans, rows, SPAN), lambda i: (0, i, 0)),
        scratch_shapes=[pltpu.VMEM((2 * STEP_GROUPS, chans, LANES), jnp.float32)],
        compiler_params=pltpu.CompilerParams(vmem_limit_bytes=VMEM_LIMIT),
        cost_estimate=pl.CostEstimate(
            flops=8_000_000_000, bytes_accessed=13_000_000, transcendentals=0
        ),
    )(own, near, far_odd, far_even)


def late_kernel(
    gram_steps,
    reach_ref,
    own_ref,
    near_ref,
    far_odd_ref,
    far_even_ref,
    early_ref,
    lag_ref,
    out_ref,
    cross,
    turned,
    wide,
):
    chans = own_ref.shape[0]
    step = pl.program_id(0)

    @pl.when(step < gram_steps)
    def _():
        def store(g, products):
            start = pl.multiple_of((step * STEP_GROUPS + g) * 2 * GROUP, 2 * GROUP)
            cross[:, pl.ds(start, 2 * GROUP), :] = products

        gram(own_ref, near_ref, far_odd_ref, far_even_ref, wide, store)

    @pl.when(step >= gram_steps)
    def _():
        depth = early_ref.shape[1]
        base = (step - gram_steps) * STEP_CHANS
        for j in range(STEP_CHANS):
            c = base + j
            lagged = jnp.dot(lag_ref[:, :depth], early_ref[j], preferred_element_type=jnp.float32)
            lagged = lagged + jnp.dot(
                lag_ref[:, depth:], cross[c], preferred_element_type=jnp.float32
            )
            start = (chans - c) * PITCH + j
            for p in range(2):
                part = lagged[p * LANES : (p + 1) * LANES].T
                if part.shape[1] < LANES:
                    rest = jnp.zeros((SPAN, LANES - part.shape[1]), jnp.float32)
                    part = jnp.concatenate([part, rest], axis=1)
                turned[p, pl.ds(start, SPAN, stride=PITCH), :] = part
        row = lax.broadcasted_iota(jnp.int32, (STEP_CHANS, LANES), 0)
        reach = jnp.zeros((STEP_CHANS, LANES), jnp.int32)
        for j in range(STEP_CHANS):
            reach = jnp.where(row == j, reach_ref[base + j], reach)
        for k in range(R + 1):
            start = (chans + k) * PITCH
            for p in range(2):
                width = min(LANES, LAGS - p * LANES)
                part = jnp.where(reach >= k, turned[p, start : start + STEP_CHANS, :], 0.0)
                out_ref[k, :, p * LANES : p * LANES + width] = part[:, :width].astype(jnp.bfloat16)


def late_correlate(windows, reach, own, near, far_odd, far_even, early):
    chans, columns = own.shape
    gram_steps = columns // COLUMNS
    depth = early.shape[1]
    block = pl.BlockSpec((chans, COLUMNS), lambda i: (0, jnp.minimum(i, gram_steps - 1)))

    def later(i):
        return jnp.maximum(i - gram_steps, 0)

    def kernel(*refs):
        late_kernel(gram_steps, *refs)

    turned = pl.pallas_call(
        kernel,
        grid=(gram_steps + chans // STEP_CHANS,),
        out_shape=jax.ShapeDtypeStruct((R + 1, chans, LAGS), jnp.bfloat16),
        in_specs=[pl.BlockSpec(memory_space=pltpu.SMEM)]
        + [block] * 4
        + [pl.BlockSpec((STEP_CHANS, depth, SPAN), lambda i: (later(i), 0, 0))]
        + [pl.BlockSpec(memory_space=pltpu.VMEM)],
        out_specs=pl.BlockSpec((R + 1, STEP_CHANS, LAGS), lambda i: (0, later(i), 0)),
        scratch_shapes=[
            pltpu.VMEM((chans, 2 * F - depth, SPAN), jnp.bfloat16),
            pltpu.VMEM((2, (chans + SPAN) * PITCH, LANES), jnp.float32),
            pltpu.VMEM((2 * STEP_GROUPS, chans, LANES), jnp.float32),
        ],
        compiler_params=pltpu.CompilerParams(vmem_limit_bytes=VMEM_LIMIT),
        cost_estimate=pl.CostEstimate(
            flops=12_000_000_000, bytes_accessed=20_000_000, transcendentals=0
        ),
    )(
        reach,
        own,
        near,
        far_odd,
        far_even,
        early,
        jnp.asarray(lag_rows(windows)),
    )
    return jnp.transpose(turned, (1, 0, 2))


def follow_kernel(value_ref, near_ref, far_ref, out_ref):
    pass


def follow(value, near, far):
    return pl.pallas_call(
        follow_kernel,
        out_shape=jax.ShapeDtypeStruct(value.shape, value.dtype),
        in_specs=[pl.BlockSpec(memory_space=pl.ANY)] * 3,
        out_specs=pl.BlockSpec(memory_space=pl.ANY),
        input_output_aliases={0: 0},
    )(value, near, far)


def neighbours(own):
    count = lax.axis_size("chan")
    near = lax.ppermute(own, "chan", [(i, i - 1) for i in range(1, count)])
    far_odd = lax.ppermute(own, "chan", [(i, i - 2) for i in range(3, count, 2)])
    return near, far_odd


def relayed(near):
    count = lax.axis_size("chan")
    return lax.ppermute(near, "chan", [(i, i - 1) for i in range(1, count, 2)])


def local(traces, quality, reach):
    windows = traces.shape[1]
    first = whiten(traces, quality, 0)
    near, far_odd = neighbours(first)
    second = whiten(traces, quality, LANES)
    next_near, next_odd = neighbours(second)
    near = follow(near, second, second)
    early = early_cross(first, near, far_odd, relayed(near))
    near = follow(next_near, early, early)
    return late_correlate(windows, reach, second, near, next_odd, relayed(near), early)


def solution(mesh):
    return jax.shard_map(
        local,
        mesh=mesh,
        in_specs=(P(("day", "chan"), None, None), P(("day", "chan"), None), P(("day", "chan"))),
        out_specs=P(("day", "chan"), None, None),
        check_vma=False,
    )
```

```python
import math

import jax
import jax.numpy as jnp
import numpy as np
from jax import lax
from jax.experimental import pallas as pl
from jax.experimental.pallas import tpu as pltpu
from jax.sharding import PartitionSpec as P

R = 160
S = 1500
F = 256
HALF_SMOOTH = 32
LAG = 100
LAGS = 2 * LAG + 1
LAG_ROWS = -(-LAGS // 16) * 16
LANES = 128
PIECES = -(-S // LANES)
GROUP = 8
GROUPS = F // GROUP
SPAN = 256
STEP_GROUPS = 4
STEP_CHANS = 16
PITCH = STEP_CHANS + 1
COLUMNS = 1024
WHITEN_CHANS = 16
VMEM_LIMIT = 32 * 1024 * 1024
WHITEN_VMEM = 56 * 1024 * 1024

eps = 1e-06


def dft_columns(first):
    times = np.arange(S, dtype=np.int32)
    own = first + HALF_SMOOTH + np.arange(LANES)
    sides = first + np.concatenate([np.arange(HALF_SMOOTH), LANES + HALF_SMOOTH + np.arange(HALF_SMOOTH)])

    def columns(bins):
        phase = times[:, None] * (1 + bins[None, :]).astype(np.int32) % S
        angle = np.float32(2.0 * math.pi / S) * phase.astype(np.float32)
        rest = ((0, PIECES * LANES - S), (0, LANES - bins.size))
        return [np.pad(part, rest) for part in (np.cos(angle), -np.sin(angle))]

    return np.concatenate(columns(own) + columns(sides), axis=1).astype(jnp.bfloat16)


def band_columns():
    rows = np.arange(LANES + 2 * HALF_SMOOTH)
    order = np.concatenate([rows[HALF_SMOOTH:-HALF_SMOOTH], rows[:HALF_SMOOTH], rows[-HALF_SMOOTH:]])
    outer = np.arange(LANES)[None, :]
    inside = (order[:, None] >= outer) & (order[:, None] <= outer + 2 * HALF_SMOOTH)
    return np.pad(inside, ((0, LANES - 2 * HALF_SMOOTH), (0, 0))).astype(jnp.bfloat16)


def lag_rows(windows):
    bins = 1 + HALF_SMOOTH + np.arange(F, dtype=np.int32)
    shifts = np.arange(LAGS, dtype=np.int32) - LAG
    phase = shifts[:, None] * bins[None, :] % S
    angle = np.float32(2.0 * math.pi / S) * phase.astype(np.float32)
    both = np.stack([np.cos(angle), -np.sin(angle)], axis=1).astype(jnp.bfloat16)
    both = both.reshape(LAGS, 2, GROUPS, GROUP).transpose(0, 2, 1, 3).reshape(LAGS, 2 * F)
    scale = np.float32(1.0 / (windows * math.sqrt(F)))
    both = (both.astype(np.float32) * scale).astype(jnp.bfloat16)
    return np.concatenate([both, np.zeros((LAG_ROWS - LAGS, 2 * F), jnp.bfloat16)], axis=0)


def whiten_kernel(traces_ref, quality_ref, dft_ref, band_ref, out_ref, wide):
    chans, windows, samples = traces_ref.shape
    pitch = windows + 1
    rows = traces_ref[...].reshape(chans * windows, samples)
    rest = jnp.zeros((chans * windows, PIECES * LANES - samples), jnp.bfloat16)
    rows = jnp.concatenate([rows, rest], axis=1)
    spectra = jnp.dot(rows, dft_ref[...], preferred_element_type=jnp.float32)
    own = [spectra[:, :LANES], spectra[:, LANES : 2 * LANES]]
    sides = [spectra[:, 2 * LANES : 3 * LANES], spectra[:, 3 * LANES :]]
    amplitude = jnp.concatenate(
        [jnp.sqrt(real * real + imag * imag) for real, imag in (own, sides)], axis=1
    )
    high = amplitude.astype(jnp.bfloat16)
    low = (amplitude - high.astype(jnp.float32)).astype(jnp.bfloat16)
    smooth = jnp.dot(high, band_ref[...], preferred_element_type=jnp.float32)
    smooth = smooth + jnp.dot(low, band_ref[...], preferred_element_type=jnp.float32)
    lane = lax.broadcasted_iota(jnp.int32, quality_ref.shape, 1) - pl.program_id(0) * chans
    quality = quality_ref[...].astype(jnp.float32)
    usable = [
        jnp.sum(jnp.where(lane == c, quality, 0.0), axis=1, keepdims=True) for c in range(chans)
    ]
    usable = jnp.concatenate([jnp.broadcast_to(u, (windows, LANES)) for u in usable], axis=0)
    scale = usable / (smooth * (1.0 / (2 * HALF_SMOOTH + 1)) + eps)
    place = lax.broadcasted_iota(jnp.int32, (chans, LANES), 1) // GROUP
    for i in range(2):
        value = own[i] * scale
        for c in range(chans):
            wide[i, c * pitch : c * pitch + windows, :] = value[c * windows : (c + 1) * windows]
        turned = []
        for n in range(windows):
            w = (windows - n) % windows
            turned.append(pltpu.roll(wide[i, pl.ds(w, chans, stride=pitch), :], w * GROUP, 1))
        shift = 1
        while shift < windows:
            moves = (place // shift) % 2 == 1
            turned = [
                jnp.where(moves, turned[(n - shift) % windows], turned[n]) for n in range(windows)
            ]
            shift *= 2
        for g in range(windows):
            start = (2 * g + i) * LANES
            out_ref[:, start : start + LANES] = turned[g].astype(jnp.bfloat16)


def whiten(traces, quality, first):
    chans, windows, _ = traces.shape
    columns = 2 * LANES * windows
    whole = pl.BlockSpec(memory_space=pltpu.VMEM)
    return pl.pallas_call(
        whiten_kernel,
        grid=(chans // WHITEN_CHANS,),
        out_shape=jax.ShapeDtypeStruct((chans, columns), jnp.bfloat16),
        in_specs=[
            pl.BlockSpec((WHITEN_CHANS, windows, S), lambda i: (i, 0, 0)),
            whole,
            whole,
            whole,
        ],
        out_specs=pl.BlockSpec((WHITEN_CHANS, columns), lambda i: (i, 0)),
        scratch_shapes=[pltpu.VMEM((2, WHITEN_CHANS * (windows + 1), LANES), jnp.float32)],
        compiler_params=pltpu.CompilerParams(vmem_limit_bytes=WHITEN_VMEM),
        cost_estimate=pl.CostEstimate(
            flops=8 * chans * windows * S * LANES, bytes_accessed=8_000_000, transcendentals=0
        ),
    )(traces, quality.T, jnp.asarray(dft_columns(first)), jnp.asarray(band_columns()))


def gram(own_ref, near_ref, far_odd_ref, far_even_ref, wide, store):
    chans = own_ref.shape[0]
    depth = own_ref.shape[1] // STEP_GROUPS
    half = depth // 2
    spot = lax.broadcasted_iota(jnp.int32, (GROUP, half), 1) % GROUP
    row = lax.broadcasted_iota(jnp.int32, (GROUP, half), 0)
    mask = spot == row
    for g in range(STEP_GROUPS):
        columns = slice(g * depth, (g + 1) * depth)
        own = own_ref[:, columns]
        far = far_odd_ref[:, columns] + far_even_ref[:, columns]
        fill = jnp.zeros((SPAN - 3 * chans, depth), jnp.bfloat16)
        others = jnp.concatenate([own, near_ref[:, columns], far, fill], axis=0)
        value = own.astype(jnp.float32)
        wide[2 * g] = value[:, :half]
        wide[2 * g + 1] = value[:, half:]
        left = []
        for c in range(chans):
            real = jnp.broadcast_to(wide[2 * g, c : c + 1, :], (GROUP, half))
            imag = jnp.broadcast_to(wide[2 * g + 1, c : c + 1, :], (GROUP, half))
            real = jnp.where(mask, real, 0.0)
            imag = jnp.where(mask, imag, 0.0)
            upper = jnp.concatenate([real, imag], axis=0).astype(jnp.bfloat16)
            lower = jnp.concatenate([imag, -real], axis=0).astype(jnp.bfloat16)
            left.append(jnp.concatenate([upper, lower], axis=1))
        products = lax.dot_general(
            jnp.concatenate(left, axis=0),
            others,
            (((1,), (1,)), ((), ())),
            preferred_element_type=jnp.float32,
        )
        store(g, products.astype(jnp.bfloat16).reshape(chans, 2 * GROUP, SPAN))


def early_kernel(own_ref, near_ref, far_odd_ref, far_even_ref, cross_ref, wide):
    def store(g, products):
        cross_ref[:, g * 2 * GROUP : (g + 1) * 2 * GROUP, :] = products

    gram(own_ref, near_ref, far_odd_ref, far_even_ref, wide, store)


def early_cross(own, near, far_odd, far_even):
    chans, columns = own.shape
    steps = columns // COLUMNS
    block = pl.BlockSpec((chans, COLUMNS), lambda i: (0, i))
    rows = STEP_GROUPS * 2 * GROUP
    return pl.pallas_call(
        early_kernel,
        grid=(steps,),
        out_shape=jax.ShapeDtypeStruct((chans, steps * rows, SPAN), jnp.bfloat16),
        in_specs=[block] * 4,
        out_specs=pl.BlockSpec((chans, rows, SPAN), lambda i: (0, i, 0)),
        scratch_shapes=[pltpu.VMEM((2 * STEP_GROUPS, chans, LANES), jnp.float32)],
        compiler_params=pltpu.CompilerParams(vmem_limit_bytes=VMEM_LIMIT),
        cost_estimate=pl.CostEstimate(
            flops=8_000_000_000, bytes_accessed=13_000_000, transcendentals=0
        ),
    )(own, near, far_odd, far_even)


def late_kernel(
    gram_steps,
    reach_ref,
    own_ref,
    near_ref,
    far_odd_ref,
    far_even_ref,
    early_ref,
    lag_ref,
    out_ref,
    cross,
    turned,
    wide,
):
    chans = own_ref.shape[0]
    step = pl.program_id(0)

    @pl.when(step < gram_steps)
    def _():
        def store(g, products):
            start = pl.multiple_of((step * STEP_GROUPS + g) * 2 * GROUP, 2 * GROUP)
            cross[:, pl.ds(start, 2 * GROUP), :] = products

        gram(own_ref, near_ref, far_odd_ref, far_even_ref, wide, store)

    @pl.when(step >= gram_steps)
    def _():
        depth = early_ref.shape[1]
        base = (step - gram_steps) * STEP_CHANS
        for j in range(STEP_CHANS):
            c = base + j
            lagged = jnp.dot(lag_ref[:, :depth], early_ref[j], preferred_element_type=jnp.float32)
            lagged = lagged + jnp.dot(
                lag_ref[:, depth:], cross[c], preferred_element_type=jnp.float32
            )
            start = (chans - c) * PITCH + j
            for p in range(2):
                part = lagged[p * LANES : (p + 1) * LANES].T
                if part.shape[1] < LANES:
                    rest = jnp.zeros((SPAN, LANES - part.shape[1]), jnp.float32)
                    part = jnp.concatenate([part, rest], axis=1)
                turned[p, pl.ds(start, SPAN, stride=PITCH), :] = part
        row = lax.broadcasted_iota(jnp.int32, (STEP_CHANS, LANES), 0)
        reach = jnp.zeros((STEP_CHANS, LANES), jnp.int32)
        for j in range(STEP_CHANS):
            reach = jnp.where(row == j, reach_ref[base + j], reach)
        for k in range(R + 1):
            start = (chans + k) * PITCH
            for p in range(2):
                width = min(LANES, LAGS - p * LANES)
                part = jnp.where(reach >= k, turned[p, start : start + STEP_CHANS, :], 0.0)
                out_ref[k, :, p * LANES : p * LANES + width] = part[:, :width].astype(jnp.bfloat16)


def late_correlate(windows, reach, own, near, far_odd, far_even, early):
    chans, columns = own.shape
    gram_steps = columns // COLUMNS
    depth = early.shape[1]
    block = pl.BlockSpec((chans, COLUMNS), lambda i: (0, jnp.minimum(i, gram_steps - 1)))

    def later(i):
        return jnp.maximum(i - gram_steps, 0)

    def kernel(*refs):
        late_kernel(gram_steps, *refs)

    turned = pl.pallas_call(
        kernel,
        grid=(gram_steps + chans // STEP_CHANS,),
        out_shape=jax.ShapeDtypeStruct((R + 1, chans, LAGS), jnp.bfloat16),
        in_specs=[pl.BlockSpec(memory_space=pltpu.SMEM)]
        + [block] * 4
        + [pl.BlockSpec((STEP_CHANS, depth, SPAN), lambda i: (later(i), 0, 0))]
        + [pl.BlockSpec(memory_space=pltpu.VMEM)],
        out_specs=pl.BlockSpec((R + 1, STEP_CHANS, LAGS), lambda i: (0, later(i), 0)),
        scratch_shapes=[
            pltpu.VMEM((chans, 2 * F - depth, SPAN), jnp.bfloat16),
            pltpu.VMEM((2, (chans + SPAN) * PITCH, LANES), jnp.float32),
            pltpu.VMEM((2 * STEP_GROUPS, chans, LANES), jnp.float32),
        ],
        compiler_params=pltpu.CompilerParams(vmem_limit_bytes=VMEM_LIMIT),
        cost_estimate=pl.CostEstimate(
            flops=12_000_000_000, bytes_accessed=20_000_000, transcendentals=0
        ),
    )(
        reach,
        own,
        near,
        far_odd,
        far_even,
        early,
        jnp.asarray(lag_rows(windows)),
    )
    return jnp.transpose(turned, (1, 0, 2))


def follow_kernel(value_ref, near_ref, far_ref, out_ref):
    pass


def follow(value, near, far):
    return pl.pallas_call(
        follow_kernel,
        out_shape=jax.ShapeDtypeStruct(value.shape, value.dtype),
        in_specs=[pl.BlockSpec(memory_space=pl.ANY)] * 3,
        out_specs=pl.BlockSpec(memory_space=pl.ANY),
        input_output_aliases={0: 0},
    )(value, near, far)


def neighbours(own):
    count = lax.axis_size("chan")
    near = lax.ppermute(own, "chan", [(i, i - 1) for i in range(1, count)])
    far_odd = lax.ppermute(own, "chan", [(i, i - 2) for i in range(3, count, 2)])
    return near, far_odd


def relayed(near):
    count = lax.axis_size("chan")
    return lax.ppermute(near, "chan", [(i, i - 1) for i in range(1, count, 2)])


def local(traces, quality, reach):
    windows = traces.shape[1]
    first = whiten(traces, quality, 0)
    near, far_odd = neighbours(first)
    second = whiten(traces, quality, LANES)
    next_near, next_odd = neighbours(second)
    near = follow(near, second, second)
    early = early_cross(first, near, far_odd, relayed(near))
    near = follow(next_near, early, early)
    return late_correlate(windows, reach, second, near, next_odd, relayed(near), early)


def solution(mesh):
    return jax.shard_map(
        local,
        mesh=mesh,
        in_specs=(P(("day", "chan"), None, None), P(("day", "chan"), None), P(("day", "chan"))),
        out_specs=P(("day", "chan"), None, None),
        check_vma=False,
    )
```
